32 devices in a mesh: grp: 4 (over y, x), seq: 4 (over z), mlp: 2 (over core).
Axes of the slice: x: 2, y: 2, z: 4, core: 2. Of those that a mesh axis runs over, the one named last changes fastest.
Arguments:
- queries: bfloat16 [16, 4, 4096], P('grp'), may hold values from -6 to 6
- new_keys: bfloat16 [16, 4, 4096], P(('grp', 'seq')), may hold values from -6 to 6
- new_values: bfloat16 [16, 4, 4096], P(('grp', 'seq')), may hold values from -6 to 6
- prefix_keys: bfloat16 [4, 2048, 4096], P('grp', ('seq', 'mlp')), may hold values from -250 to 250
- prefix_values: bfloat16 [4, 2048, 4096], P('grp', ('seq', 'mlp')), may hold values from -6 to 6
- tail_keys: bfloat16 [16, 256, 4096], P(('grp', 'seq'), 'mlp'), may hold values from -6 to 6
- tail_values: bfloat16 [16, 256, 4096], P(('grp', 'seq'), 'mlp'), may hold values from -6 to 6
- prefix_len: int32 [4], P('grp'), may hold values from 1 to 2048, as said below
- tail_len: int32 [16], P('grp'), may hold values from 0 to 256, as said below
- resid: bfloat16 [16, 4, 4096], P('grp', None, ('seq', 'mlp')), may hold values from -12 to 12
- w_out: bfloat16 [4096, 4096], P(None, ('seq', 'mlp')), may hold values from -0.09375 to 0.09375
- ln_gain: bfloat16 [4096], P(('seq', 'mlp')), may hold values from 0.25 to 1.75
- w_up: bfloat16 [4096, 16384], P(('seq', 'mlp'), 'grp'), may hold values from -0.09375 to 0.09375
- w_down: bfloat16 [16384, 4096], P('grp', ('seq', 'mlp')), may hold values from -0.046875 to 0.046875
Outputs:
- out: float32 [16, 4, 4096], P('grp', None, ('seq', 'mlp'))
The draws below stay inside these ranges and needn't reach their ends.
Inputs may be any that keep to these rules, and one draw needn't show every extreme that they name: `prefix_len`: every group's live prefix is 1 to 2048 slots; in every draw some group's prefix fills all 2048 slots. `tail_len`: A request's live tail is 0 to 256 slots; in every draw some request's tail fills all 256 slots.
All inputs are finite; a program needn't handle non-finite values.
Results may differ from the reference program's by a relative error of at most 0.0075.
Values may be sent and summed in bfloat16 or wider, within the bound.
A program may use at most 128 MiB of HBM per device.

```python
import math
import jax
import jax.numpy as jnp
from jax import lax

D = 4096
H = 32
HD = 128
FF = 16384
STEPS = 4
GROUPS = 4
GROUP_REQ = 4
REQS = 16
PREFIX = 2048
TAIL = 256


def draw_prefix_keys(key, part):
    drawn = jnp.clip(jax.random.normal(key, (GROUPS, PREFIX, D), jnp.float32), -6.0, 6.0)
    return drawn.astype(jnp.bfloat16)


def draw_resid(key, part):
    row_draw = jax.random.uniform(jax.random.fold_in(key, 1), (REQS, STEPS, 1), jnp.float32)
    col_draw = jax.random.uniform(jax.random.fold_in(key, 2), (D,), jnp.float32)
    trend = jnp.power(3.0, jnp.arange(D, dtype=jnp.float32) / (D - 1) - 0.5)
    row_scale = jnp.power(10.0, row_draw * 0.5 - 0.25)
    col_scale = jnp.power(10.0, col_draw * 0.5 - 0.25) * trend
    noise = jnp.clip(jax.random.normal(key, (REQS, STEPS, D), jnp.float32), -5.0, 5.0)
    return (0.25 * noise * row_scale * col_scale).astype(jnp.bfloat16)


def draw_prefix_len(key, part):
    lengths = jax.random.randint(key, (GROUPS,), 1, PREFIX + 1)
    longest = jax.random.randint(jax.random.fold_in(key, 5), (), 0, GROUPS)
    return jnp.where(jnp.arange(GROUPS) == longest, PREFIX, lengths).astype(jnp.int32)


def draw_tail_len(key, part):
    lengths = jax.random.randint(key, (REQS,), 0, TAIL + 1)
    longest = jax.random.randint(jax.random.fold_in(key, 6), (), 0, REQS)
    return jnp.where(jnp.arange(REQS) == longest, TAIL, lengths).astype(jnp.int32)


def level_of(stream_key, shape, cuts, least, largest):
    def one(dim, blocks):
        steps = jax.random.uniform(jax.random.fold_in(jax.random.fold_in(stream_key, 6), dim), (blocks,), jnp.float32, least / len(cuts), largest / len(cuts))
        return jnp.repeat(jnp.exp(steps), shape[dim] // blocks).reshape((-1,) + (1,) * (len(shape) - dim - 1))

    gain = one(*cuts[0])
    for cut in cuts[1:]:
        gain = gain * one(*cut)
    return gain


def normal_values(rng, shape, scale, bound, cuts=(), kind=jnp.bfloat16):
    values = jax.random.normal(rng, shape, jnp.float32) * scale
    if len(cuts) > 0:
        values = level_of(rng, shape, cuts, -0.22, 0.18) * values
    return jnp.clip(values, min=-bound, max=bound).astype(kind)


def setup_inputs(seed: int = 0) -> dict:
    key_of = jax.random.split(jax.random.key(seed), 15)
    return {
        "queries": normal_values(key_of[0], (REQS, STEPS, D), 1.0, 6.0, ((0, 4),)),
        "new_keys": normal_values(key_of[1], (REQS, STEPS, D), 1.0, 6.0, ((0, 16),)),
        "new_values": normal_values(key_of[2], (REQS, STEPS, D), 1.0, 6.0, ((0, 16),)),
        "prefix_keys": draw_prefix_keys(jax.random.fold_in(key_of[14], 71), 0),
        "prefix_values": normal_values(key_of[4], (GROUPS, PREFIX, D), 1.0, 6.0, ((0, 4), (1, 8))),
        "tail_keys": normal_values(key_of[5], (REQS, TAIL, D), 1.0, 6.0, ((0, 16), (1, 2))),
        "tail_values": normal_values(key_of[6], (REQS, TAIL, D), 1.0, 6.0, ((0, 16), (1, 2))),
        "prefix_len": draw_prefix_len(jax.random.fold_in(key_of[14], 71), 0),
        "tail_len": draw_tail_len(jax.random.fold_in(key_of[14], 71), 0),
        "resid": draw_resid(jax.random.fold_in(key_of[14], 71), 0),
        "w_out": normal_values(key_of[10], (D, D), D ** -0.5, 0.09375, ((1, 8),)),
        "ln_gain": jnp.clip(1.0 + 0.15 * jax.random.normal(key_of[11], (D,), jnp.float32), 0.25, 1.75).astype(jnp.bfloat16),
        "w_up": normal_values(key_of[12], (D, FF), D ** -0.5, 0.09375, ((0, 8), (1, 4))),
        "w_down": normal_values(key_of[13], (FF, D), FF ** -0.5, 0.046875, ((0, 4), (1, 8))),
    }


NEG = -1e+30

def head_slopes(count):
    return jnp.power(2.0, -8.0 * (jnp.arange(count, dtype=jnp.float32) + 1.0) / count)

def group_attention(inputs):
    queries, new_keys, new_values, prefix_keys, prefix_values, tail_keys, tail_values, prefix_end, tail_lens = inputs
    query_heads = queries.astype(jnp.float32).reshape(GROUP_REQ, STEPS, H, HD)
    step_index = jnp.arange(STEPS, dtype=jnp.int32)
    query_pos = prefix_end + tail_lens[:, None] + step_index[None, :]
    slopes = head_slopes(H)[None, :, None, None]
    inv_scale = 1.0 / math.sqrt(HD)
    prefix_index = jnp.arange(PREFIX, dtype=jnp.int32)
    prefix_scores = jnp.einsum('rthd,khd->rhtk', query_heads, prefix_keys.astype(jnp.float32).reshape(PREFIX, H, HD)) * inv_scale
    prefix_scores = prefix_scores - slopes * (query_pos[:, None, :, None] - prefix_index[None, None, None, :]).astype(jnp.float32)
    prefix_mask = jnp.broadcast_to((prefix_index < prefix_end)[None, None, None, :], prefix_scores.shape)
    tail_index = jnp.arange(TAIL, dtype=jnp.int32)
    tail_scores = jnp.einsum('rthd,rkhd->rhtk', query_heads, tail_keys.astype(jnp.float32).reshape(GROUP_REQ, TAIL, H, HD)) * inv_scale
    tail_scores = tail_scores - slopes * (query_pos[:, None, :, None] - (prefix_end + tail_index)[None, None, None, :]).astype(jnp.float32)
    tail_mask = jnp.broadcast_to((tail_index[None, :] < tail_lens[:, None])[:, None, None, :], tail_scores.shape)
    new_scores = jnp.einsum('rthd,rkhd->rhtk', query_heads, new_keys.astype(jnp.float32).reshape(GROUP_REQ, STEPS, H, HD)) * inv_scale
    new_scores = new_scores - slopes * (query_pos[:, None, :, None] - query_pos[:, None, None, :]).astype(jnp.float32)
    new_mask = jnp.broadcast_to((step_index[None, :] <= step_index[:, None])[None, None, :, :], new_scores.shape)
    pieces = [(prefix_scores, prefix_mask), (tail_scores, tail_mask), (new_scores, new_mask)]
    row_max = lax.optimization_barrier(jnp.max(jnp.where(prefix_mask, prefix_scores, NEG), axis=-1))
    row_max = jnp.maximum(row_max, lax.optimization_barrier(jnp.max(jnp.where(tail_mask, tail_scores, NEG), axis=-1)))
    row_max = jnp.maximum(row_max, lax.optimization_barrier(jnp.max(jnp.where(new_mask, new_scores, NEG), axis=-1)))
    weight_list = [jnp.where(mask, jnp.exp(scores - row_max[..., None]), 0.0) for scores, mask in pieces]
    weight_sum = lax.optimization_barrier(jnp.sum(weight_list[0], -1)) + lax.optimization_barrier(jnp.sum(weight_list[1], -1)) + lax.optimization_barrier(jnp.sum(weight_list[2], -1))
    rounded = [lax.optimization_barrier(member.astype(jnp.bfloat16)).astype(jnp.float32) for member in weight_list]
    mixed_sum = jnp.einsum('rhtk,khd->rthd', rounded[0], prefix_values.astype(jnp.float32).reshape(PREFIX, H, HD))
    mixed_sum = mixed_sum + jnp.einsum('rhtk,rkhd->rthd', rounded[1], tail_values.astype(jnp.float32).reshape(GROUP_REQ, TAIL, H, HD))
    mixed_sum = mixed_sum + jnp.einsum('rhtk,rkhd->rthd', rounded[2], new_values.astype(jnp.float32).reshape(GROUP_REQ, STEPS, H, HD))
    attention = mixed_sum / jnp.transpose(weight_sum, (0, 2, 1))[..., None]
    return attention.astype(jnp.bfloat16).reshape(GROUP_REQ, STEPS, D)

def reference(queries, new_keys, new_values, prefix_keys, prefix_values, tail_keys, tail_values, prefix_len, tail_len, resid, w_out, ln_gain, w_up, w_down):
    grouped = (queries.reshape(GROUPS, GROUP_REQ, STEPS, D), new_keys.reshape(GROUPS, GROUP_REQ, STEPS, D), new_values.reshape(GROUPS, GROUP_REQ, STEPS, D), prefix_keys, prefix_values, tail_keys.reshape(GROUPS, GROUP_REQ, TAIL, D), tail_values.reshape(GROUPS, GROUP_REQ, TAIL, D), prefix_len, tail_len.reshape(GROUPS, GROUP_REQ))
    attention = lax.map(group_attention, grouped).reshape(REQS * STEPS, D)
    stream = resid.astype(jnp.float32).reshape(REQS * STEPS, D) + jnp.dot(attention, w_out, preferred_element_type=jnp.float32)
    row_mean = lax.optimization_barrier(jnp.mean(stream, axis=1))
    row_var = lax.optimization_barrier(jnp.mean(stream * stream, axis=1)) - row_mean * row_mean
    hidden = ((stream - row_mean[:, None]) * lax.rsqrt(row_var[:, None] + 1e-05) * ln_gain.astype(jnp.float32)).astype(jnp.bfloat16)
    lifted = jnp.dot(hidden, w_up, preferred_element_type=jnp.float32)
    activated = jax.nn.gelu(lifted, approximate=False).astype(jnp.bfloat16)
    result = stream + jnp.dot(activated, w_down, preferred_element_type=jnp.float32)
    return result.reshape(REQS, STEPS, D)
```

```python
import functools
import math

import jax
import jax.numpy as jnp
import numpy as np
from jax import lax
from jax.experimental import pallas as pl
from jax.experimental.pallas import tpu as pltpu
from jax.sharding import PartitionSpec as P

D = 4096
H = 32


NEG = -1e30


def merged(value, axis, join):
    pieces = jax.tree.map(lambda part: lax.all_gather(part, axis), value)
    head = jax.tree.map(lambda part: part[0], pieces)
    tail = jax.tree.map(lambda part: part[1:], pieces)
    so_far, _ = lax.scan(lambda so_far, piece: (join(so_far, piece), None), head, tail)
    return so_far


def head_slopes(count):
    return jnp.power(2.0, -8.0 * (jnp.arange(count, dtype=jnp.float32) + 1.0) / count)


def attend(query_rows, key_block, value_block, query_pos, key_pos, key_mask):
    head_count = query_rows.shape[1]
    inv_scale = 1.0 / math.sqrt(query_rows.shape[2])
    scores = (
        jnp.einsum("qhd,khd->hqk", query_rows, key_block, preferred_element_type=jnp.float32)
        * inv_scale
    )
    distance = (query_pos[:, None] - key_pos[None, :]).astype(jnp.float32)
    scores = scores - head_slopes(head_count)[:, None, None] * distance[None, :, :]
    scores = jnp.where(key_mask, scores, NEG)
    row_max = jnp.max(scores, axis=2)
    weights = jnp.where(key_mask, jnp.exp(scores - row_max[:, :, None]), 0.0)
    weight_sum = jnp.sum(weights, axis=2)
    mixed_sum = jnp.einsum(
        "hqk,khd->qhd",
        weights.astype(jnp.bfloat16),
        value_block,
        preferred_element_type=jnp.float32,
    )
    return (row_max.T, weight_sum.T, mixed_sum)


def join_parts(first, second):
    best_max = jnp.maximum(first[0], second[0])
    factor_one = jnp.exp(first[0] - best_max)
    factor_two = jnp.exp(second[0] - best_max)
    return (
        best_max,
        first[1] * factor_one + second[1] * factor_two,
        first[2] * factor_one[:, :, None] + second[2] * factor_two[:, :, None],
    )


def body(
    queries,
    new_keys,
    new_values,
    prefix_keys,
    prefix_values,
    tail_keys,
    tail_values,
    prefix_len,
    tail_len,
    resid,
    w_out,
    ln_gain,
    w_up,
    w_down,
):
    group_req, step_count, model_width = queries.shape
    head_dim = model_width // H
    row_count = group_req * step_count
    seq_index = lax.axis_index("seq")
    core_index = lax.axis_index("mlp")
    block_len = prefix_keys.shape[1]
    tail_block = tail_keys.shape[1]
    block_start = (seq_index * lax.axis_size("mlp") + core_index) * block_len
    prefix_end = prefix_len[0]
    step_index = jnp.arange(step_count, dtype=jnp.int32)
    query_pos = prefix_end + jnp.repeat(tail_len, step_count) + jnp.tile(step_index, group_req)
    query_rows = queries.reshape(row_count, H, head_dim)
    key_pos = block_start + jnp.arange(block_len, dtype=jnp.int32)
    key_live = key_pos < prefix_end
    own_len = lax.dynamic_index_in_dim(tail_len, seq_index, 0, keepdims=False)
    own_rows = lax.dynamic_slice_in_dim(query_rows, seq_index * step_count, step_count, 0)
    own_pos = prefix_end + own_len + step_index
    tail_index = core_index * tail_block + jnp.arange(tail_block, dtype=jnp.int32)
    partial_value = attend(
        query_rows,
        prefix_keys[0].reshape(block_len, H, head_dim),
        prefix_values[0].reshape(block_len, H, head_dim),
        query_pos,
        key_pos,
        key_live[None, None, :],
    )
    tail_result = attend(
        own_rows,
        tail_keys[0].reshape(tail_block, H, head_dim),
        tail_values[0].reshape(tail_block, H, head_dim),
        own_pos,
        prefix_end + tail_index,
        (tail_index < own_len)[None, None, :],
    )
    self_mask = (step_index[None, :] <= step_index[:, None]) & (core_index == 0)
    self_result = attend(
        own_rows,
        new_keys[0].reshape(step_count, H, head_dim),
        new_values[0].reshape(step_count, H, head_dim),
        own_pos,
        own_pos,
        self_mask[None, :, :],
    )
    own_slice = tuple(
        (
            lax.dynamic_slice_in_dim(member, seq_index * step_count, step_count, 0)
            for member in partial_value
        )
    )
    own_part = join_parts(join_parts(own_slice, tail_result), self_result)
    partial_value = tuple(
        (
            lax.dynamic_update_slice_in_dim(member, update, seq_index * step_count, 0)
            for member, update in zip(partial_value, own_part)
        )
    )
    row_max, weight_sum, mixed_sum = merged(
        (partial_value[0], partial_value[1], partial_value[2]), ("seq", "mlp"), join_parts
    )
    attention = (
        (mixed_sum / weight_sum[:, :, None]).astype(jnp.bfloat16).reshape(row_count, model_width)
    )
    width_block = resid.shape[2]
    stream = resid.astype(jnp.float32).reshape(row_count, width_block) + jnp.dot(
        attention, w_out, preferred_element_type=jnp.float32
    )
    row_sums, squares = lax.psum(
        (jnp.sum(stream, axis=1), jnp.sum(stream * stream, axis=1)), ("seq", "mlp")
    )
    row_mean = row_sums / D
    row_var = squares / D - row_mean * row_mean
    hidden = (
        (stream - row_mean[:, None])
        * lax.rsqrt(row_var[:, None] + 1e-05)
        * ln_gain.astype(jnp.float32)
    ).astype(jnp.bfloat16)
    lifted = jnp.dot(
        lax.all_gather(hidden, "grp", axis=0, tiled=True), w_up, preferred_element_type=jnp.float32
    )
    summed = lax.psum(lifted, ("seq", "mlp"))
    activated = jax.nn.gelu(summed, approximate=False).astype(jnp.bfloat16)
    projected = lax.psum_scatter(
        jnp.dot(activated, w_down, preferred_element_type=jnp.float32),
        "grp",
        scatter_dimension=0,
        tiled=True,
    )
    return (stream + projected).reshape(group_req, step_count, width_block)


F32 = jnp.float32
BF16 = jnp.bfloat16
LANES = 128
NEW_PAD = 16
FLOOR = -1e29
FAR = 1e33


def remote(src, dst, send_sem, recv_sem, device):
    return pltpu.make_async_remote_copy(
        src_ref=src,
        dst_ref=dst,
        send_sem=send_sem,
        recv_sem=recv_sem,
        device_id=device,
        device_id_type=pl.DeviceIdType.MESH,
    )


def layer_kernel(
    G,
    S,
    C,
    q_hbm,
    nk_hbm,
    nv_hbm,
    pk_hbm,
    pv_hbm,
    tk_hbm,
    tv_hbm,
    plen,
    tlen,
    slopes,
    resid_hbm,
    gain_ref,
    wo_hbm,
    wu_hbm,
    wd_hbm,
    out_ref,
    q_in,
    nk_in,
    nv_in,
    resid_in,
    stage,
    qbuf,
    kbuf,
    vbuf,
    dist,
    wo,
    wu,
    wd,
    o_send,
    o_recv,
    st_send,
    st_recv,
    att,
    ybuf,
    sum_send,
    sum_recv,
    hid,
    up_send,
    up_pair,
    up_zsend,
    up_zrecv,
    act,
    acc,
    proj_send,
    proj_recv,
    load_sem,
    o_ss,
    o_rs,
    st_ss,
    st_rs,
    att_ss,
    att_rs,
    sum_ss,
    sum_rs,
    hid_ss,
    hid_rs,
    pair_ss,
    pair_rs,
    zup_ss,
    zup_rs,
    act_ss,
    fwd_ss,
    act_rs,
    proj_ss,
    proj_rs,
):
    N = S * C
    grp = lax.axis_index("grp")
    seq = lax.axis_index("seq")
    core = lax.axis_index("mlp")
    me = seq * C + core
    group_req, steps, width = q_in.shape
    rows = group_req * steps
    prefix = pk_hbm.shape[1]
    tail = tk_hbm.shape[1]
    keys = kbuf.shape[0]
    block = ybuf.shape[1]
    head_dim = width // H
    heads = block // head_dim

    def peer(index):
        return {"seq": index // C, "mlp": lax.rem(index, C)}

    loads = [
        pltpu.make_async_copy(q_hbm, q_in, load_sem.at[0]),
        pltpu.make_async_copy(nk_hbm, nk_in, load_sem.at[1]),
        pltpu.make_async_copy(nv_hbm, nv_in, load_sem.at[2]),
        pltpu.make_async_copy(pk_hbm.at[0], kbuf.at[pl.ds(0, prefix)], load_sem.at[3]),
        pltpu.make_async_copy(tk_hbm.at[0], kbuf.at[pl.ds(prefix, tail)], load_sem.at[4]),
        pltpu.make_async_copy(pv_hbm.at[0], vbuf.at[pl.ds(0, prefix)], load_sem.at[5]),
        pltpu.make_async_copy(tv_hbm.at[0], vbuf.at[pl.ds(prefix, tail)], load_sem.at[6]),
        pltpu.make_async_copy(resid_hbm, resid_in, load_sem.at[7]),
    ]
    wo_load = pltpu.make_async_copy(wo_hbm, wo, load_sem.at[8])
    wu_load = pltpu.make_async_copy(wu_hbm, wu, load_sem.at[9])
    wd_load = pltpu.make_async_copy(wd_hbm, wd, load_sem.at[10])
    for load in loads:
        load.start()

    barrier = pltpu.get_barrier_semaphore()
    for k in range(1, N):
        pl.semaphore_signal(
            barrier, inc=1, device_id=peer(lax.rem(me + k, N)), device_id_type=pl.DeviceIdType.MESH
        )
    for k in range(1, G):
        pl.semaphore_signal(
            barrier,
            inc=1,
            device_id={"grp": lax.rem(grp + k, G)},
            device_id_type=pl.DeviceIdType.MESH,
        )

    row = lax.broadcasted_iota(jnp.int32, (rows, keys), 0)
    col = lax.broadcasted_iota(jnp.int32, (rows, keys), 1)
    request = row // steps
    step = row - request * steps
    prefix_end = plen[0]
    length = jnp.zeros((rows, keys), jnp.int32)
    for r in range(group_req):
        length = jnp.where(request == r, tlen[r], length)
    own = request == seq
    key_pos = me * prefix + col
    tail_pos = core * tail + col - prefix
    new_pos = col - prefix - tail
    is_prefix = col < prefix
    is_tail = jnp.logical_and(col >= prefix, col < prefix + tail)
    is_new = jnp.logical_and(col >= prefix + tail, new_pos < steps)
    apart = jnp.where(
        is_prefix,
        prefix_end + length + step - key_pos,
        jnp.where(is_tail, length + step - tail_pos, step - new_pos),
    )
    live_prefix = jnp.logical_and(is_prefix, key_pos < prefix_end)
    live_tail = jnp.logical_and(jnp.logical_and(is_tail, tail_pos < length), own)
    live_new = jnp.logical_and(
        jnp.logical_and(is_new, new_pos <= step), jnp.logical_and(own, core == 0)
    )
    live = jnp.logical_or(live_prefix, jnp.logical_or(live_tail, live_new))
    dist[...] = jnp.where(live, apart.astype(F32), FAR)

    stage[...] = jnp.zeros_like(stage)
    loads[1].wait()
    stage[0:steps, :] = nk_in[0].astype(F32)
    kbuf[prefix + tail : keys, :] = stage[...].astype(BF16)
    loads[2].wait()
    stage[0:steps, :] = nv_in[0].astype(F32)
    vbuf[prefix + tail : keys, :] = stage[...].astype(BF16)
    loads[0].wait()
    for r in range(group_req):
        stage[r * steps : (r + 1) * steps, :] = q_in[r].astype(F32)
    qbuf[...] = stage[...].astype(BF16)
    loads[7].wait()
    for r in range(group_req):
        ybuf[r * steps : (r + 1) * steps, :] = resid_in[r].astype(F32)

    for i in range(3, 7):
        loads[i].wait()
    wo_load.start()
    wu_load.start()
    wd_load.start()

    pl.semaphore_wait(barrier, N - 1 + G - 1)

    inv_scale = 1.0 / math.sqrt(head_dim)
    lane = lax.broadcasted_iota(jnp.int32, (rows, LANES), 1)

    def partials(i, carry):
        p = lax.rem(me + 1 + i, N)
        base = pl.multiple_of(p * block, block)
        stats = jnp.zeros((rows, LANES), F32)
        for j in range(heads):
            cols = pl.ds(base + j * head_dim, head_dim)
            scores = lax.dot_general(
                qbuf[:, cols], kbuf[:, cols], (((1,), (1,)), ((), ())), preferred_element_type=F32
            )
            scores = scores * inv_scale - slopes[p * heads + j] * dist[...]
            top = jnp.maximum(jnp.max(scores, axis=1, keepdims=True), FLOOR)
            weights = jnp.exp(scores - top)
            total = jnp.sum(weights, axis=1, keepdims=True)
            mixed = jnp.dot(weights.astype(BF16), vbuf[:, cols], preferred_element_type=F32)
            o_send[p, :, j * head_dim : (j + 1) * head_dim] = mixed.astype(BF16)
            stats = jnp.where(lane == j, top, stats)
            stats = jnp.where(lane == heads + j, total, stats)
        st_send[p] = stats

        @pl.when(i < N - 1)
        def _():
            remote(o_send.at[p], o_recv.at[me], o_ss.at[p], o_rs.at[me], peer(p)).start()
            remote(st_send.at[p], st_recv.at[me], st_ss.at[p], st_rs.at[me], peer(p)).start()

        return carry

    lax.fori_loop(0, N, partials, 0)
    o_recv[me] = o_send[me]
    st_recv[me] = st_send[me]

    for k in range(1, N):
        p = lax.rem(me + N - k, N)
        remote(o_send.at[p], o_recv.at[p], o_ss.at[p], o_rs.at[p], peer(p)).wait_recv()
        remote(st_send.at[p], st_recv.at[p], st_ss.at[p], st_rs.at[p], peer(p)).wait_recv()
    stats = [st_recv[i] for i in range(N)]
    best = stats[0]
    for i in range(1, N):
        best = jnp.maximum(best, stats[i])
    factors = [jnp.exp(member - best) for member in stats]
    whole = factors[0] * pltpu.roll(stats[0], LANES - heads, 1)
    for i in range(1, N):
        whole = whole + factors[i] * pltpu.roll(stats[i], LANES - heads, 1)
    for j in range(heads):
        cols = slice(j * head_dim, (j + 1) * head_dim)
        mixed = o_recv[0, :, cols].astype(F32) * factors[0][:, j : j + 1]
        for i in range(1, N):
            mixed = mixed + o_recv[i, :, cols].astype(F32) * factors[i][:, j : j + 1]
        att[me, :, cols] = (mixed / whole[:, j : j + 1]).astype(BF16)
    for k in range(1, N):
        p = lax.rem(me + k, N)
        remote(att.at[me], att.at[me], att_ss.at[p], att_rs.at[me], peer(p)).start()

    wo_load.wait()

    def out_proj(k, carry):
        p = lax.rem(me + N - k, N)

        @pl.when(k > 0)
        def _():
            remote(att.at[p], att.at[p], att_ss.at[p], att_rs.at[p], peer(p)).wait_recv()

        piece = pl.ds(pl.multiple_of(p * block, block), block)
        ybuf[...] += jnp.dot(att[p], wo[piece, :], preferred_element_type=F32)
        return carry

    lax.fori_loop(0, N, out_proj, 0)

    y = ybuf[...]
    sums = jnp.where(lane == 0, jnp.sum(y, axis=1, keepdims=True), 0.0)
    sums = jnp.where(lane == 1, jnp.sum(y * y, axis=1, keepdims=True), sums)
    sum_send[...] = sums
    for k in range(1, N):
        p = lax.rem(me + k, N)
        remote(sum_send, sum_recv.at[me], sum_ss.at[p], sum_rs.at[me], peer(p)).start()
    sum_recv[me] = sums
    for k in range(1, N):
        p = lax.rem(me + N - k, N)
        remote(sum_send, sum_recv.at[p], sum_ss.at[p], sum_rs.at[p], peer(p)).wait_recv()
    sums = jnp.sum(sum_recv[...], axis=0)
    mean = sums[:, 0:1] / width
    var = sums[:, 1:2] / width - mean * mean
    hidden = (y - mean) * lax.rsqrt(var + 1e-05) * gain_ref[...].astype(F32)
    mine = pl.ds(pl.multiple_of(grp * rows, rows), rows)
    hid[mine, :] = hidden.astype(BF16)
    for k in range(1, G):
        g = lax.rem(grp + k, G)
        remote(hid.at[mine], hid.at[mine], hid_ss.at[g], hid_rs.at[grp], {"grp": g}).start()
    wu_load.wait()
    for k in range(1, G):
        g = lax.rem(grp + G - k, G)
        theirs = pl.ds(pl.multiple_of(g * rows, rows), rows)
        remote(hid.at[theirs], hid.at[theirs], hid_ss.at[g], hid_rs.at[g], {"grp": g}).wait_recv()

    other = 1 - core

    def lift(index):
        piece = pl.ds(pl.multiple_of(index * act.shape[2], act.shape[2]), act.shape[2])
        return jnp.dot(hid[...], wu[:, piece], preferred_element_type=F32)

    def pair_blocks(k, carry):
        z = lax.rem(seq + 1 + k, S)
        up_send[z] = lift(z * C + other).astype(BF16)
        remote(up_send.at[z], up_pair.at[z], pair_ss.at[z], pair_rs.at[z], {"mlp": other}).start()
        return carry

    lax.fori_loop(0, S, pair_blocks, 0)

    def z_blocks(k, carry):
        z = lax.rem(seq + 1 + k, S)
        part = lift(z * C + core)
        remote(
            up_send.at[z], up_pair.at[z], pair_ss.at[z], pair_rs.at[z], {"mlp": other}
        ).wait_recv()
        part = part + up_pair[z].astype(F32)

        @pl.when(k < S - 1)
        def _():
            up_zsend[z] = part.astype(BF16)
            remote(
                up_zsend.at[z], up_zrecv.at[seq], zup_ss.at[z], zup_rs.at[seq], {"seq": z}
            ).start()

        @pl.when(k == S - 1)
        def _():
            acc[...] = part

        return carry

    lax.fori_loop(0, S, z_blocks, 0)
    lifted = acc[...]
    for k in range(1, S):
        z = lax.rem(seq + S - k, S)
        remote(
            up_zsend.at[z], up_zrecv.at[z], zup_ss.at[z], zup_rs.at[z], {"seq": z}
        ).wait_recv()
        lifted = lifted + up_zrecv[z].astype(F32)
    act[me] = (0.5 * lifted * (1.0 + lax.erf(lifted * math.sqrt(0.5)))).astype(BF16)

    for k in range(1, S):
        z = lax.rem(seq + k, S)
        remote(act.at[me], act.at[me], act_ss.at[z], act_rs.at[me], {"seq": z}).start()
    remote(act.at[me], act.at[me], fwd_ss.at[seq], act_rs.at[me], {"mlp": other}).start()

    wd_load.wait()

    def lower(index):
        piece = pl.ds(pl.multiple_of(index * act.shape[2], act.shape[2]), act.shape[2])
        return jnp.dot(act[index], wd[piece, :], preferred_element_type=F32)

    acc[...] = lower(me)

    def down(k, carry):
        z = lax.rem(seq + S - k, S)
        near = z * C + core
        far = z * C + other

        @pl.when(k > 0)
        def _():
            remote(act.at[near], act.at[near], act_ss.at[z], act_rs.at[near], {"seq": z}).wait_recv()
            remote(act.at[near], act.at[near], fwd_ss.at[z], act_rs.at[near], {"mlp": other}).start()
            acc[...] += lower(near)

        remote(act.at[far], act.at[far], fwd_ss.at[z], act_rs.at[far], {"mlp": other}).wait_recv()
        acc[...] += lower(far)
        return carry

    lax.fori_loop(0, S, down, 0)

    for k in range(1, G):
        g = lax.rem(grp + k, G)
        theirs = pl.ds(pl.multiple_of(g * rows, rows), rows)
        proj_send[g] = acc[theirs, :].astype(BF16)
        remote(
            proj_send.at[g], proj_recv.at[grp], proj_ss.at[g], proj_rs.at[grp], {"grp": g}
        ).start()
    total = ybuf[...] + acc[mine, :]
    for k in range(1, G):
        g = lax.rem(grp + G - k, G)
        remote(
            proj_send.at[g], proj_recv.at[g], proj_ss.at[g], proj_rs.at[g], {"grp": g}
        ).wait_recv()
        total = total + proj_recv[g].astype(F32)
    ybuf[...] = total
    for r in range(group_req):
        out_ref[r] = ybuf[r * steps : (r + 1) * steps, :]

    for k in range(1, N):
        p = lax.rem(me + k, N)
        remote(o_send.at[p], o_recv.at[me], o_ss.at[p], o_rs.at[me], peer(p)).wait_send()
        remote(st_send.at[p], st_recv.at[me], st_ss.at[p], st_rs.at[me], peer(p)).wait_send()
        remote(att.at[me], att.at[me], att_ss.at[p], att_rs.at[me], peer(p)).wait_send()
        remote(sum_send, sum_recv.at[me], sum_ss.at[p], sum_rs.at[me], peer(p)).wait_send()
    for k in range(1, G):
        g = lax.rem(grp + k, G)
        remote(hid.at[mine], hid.at[mine], hid_ss.at[g], hid_rs.at[grp], {"grp": g}).wait_send()
        remote(
            proj_send.at[g], proj_recv.at[grp], proj_ss.at[g], proj_rs.at[grp], {"grp": g}
        ).wait_send()
    for z in range(S):
        remote(
            up_send.at[z], up_pair.at[z], pair_ss.at[z], pair_rs.at[z], {"mlp": other}
        ).wait_send()
        near = z * C + core
        remote(act.at[near], act.at[near], fwd_ss.at[z], act_rs.at[near], {"mlp": other}).wait_send()
    for k in range(1, S):
        z = lax.rem(seq + k, S)
        remote(
            up_zsend.at[z], up_zrecv.at[seq], zup_ss.at[z], zup_rs.at[seq], {"seq": z}
        ).wait_send()
        remote(act.at[me], act.at[me], act_ss.at[z], act_rs.at[me], {"seq": z}).wait_send()


def fused(
    G,
    S,
    C,
    queries,
    new_keys,
    new_values,
    prefix_keys,
    prefix_values,
    tail_keys,
    tail_values,
    prefix_len,
    tail_len,
    resid,
    w_out,
    ln_gain,
    w_up,
    w_down,
):
    group_req, steps, width = queries.shape
    rows = group_req * steps
    N = S * C
    block = resid.shape[2]
    lifted = w_up.shape[1] // N
    keys = prefix_keys.shape[1] + tail_keys.shape[1] + NEW_PAD
    slopes = jnp.asarray(np.power(2.0, -8.0 * (np.arange(H) + 1.0) / H).astype(np.float32))
    dma = pltpu.SemaphoreType.DMA
    hbm = pl.BlockSpec(memory_space=pl.ANY)
    smem = pl.BlockSpec(memory_space=pltpu.SMEM)
    vmem = pl.BlockSpec(memory_space=pltpu.VMEM)
    return pl.pallas_call(
        functools.partial(layer_kernel, G, S, C),
        out_shape=jax.ShapeDtypeStruct((group_req, steps, block), F32),
        in_specs=[hbm] * 7 + [smem] * 3 + [hbm, vmem] + [hbm] * 3,
        out_specs=vmem,
        scratch_shapes=[
            pltpu.VMEM(queries.shape, BF16),
            pltpu.VMEM(new_keys.shape, BF16),
            pltpu.VMEM(new_values.shape, BF16),
            pltpu.VMEM(resid.shape, BF16),
            pltpu.VMEM((rows, width), F32),
            pltpu.VMEM((rows, width), BF16),
            pltpu.VMEM((keys, width), BF16),
            pltpu.VMEM((keys, width), BF16),
            pltpu.VMEM((rows, keys), F32),
            pltpu.VMEM(w_out.shape, BF16),
            pltpu.VMEM(w_up.shape, BF16),
            pltpu.VMEM(w_down.shape, BF16),
            pltpu.VMEM((N, rows, block), BF16),
            pltpu.VMEM((N, rows, block), BF16),
            pltpu.VMEM((N, rows, LANES), F32),
            pltpu.VMEM((N, rows, LANES), F32),
            pltpu.VMEM((N, rows, block), BF16),
            pltpu.VMEM((rows, block), F32),
            pltpu.VMEM((rows, LANES), F32),
            pltpu.VMEM((N, rows, LANES), F32),
            pltpu.VMEM((G * rows, block), BF16),
            pltpu.VMEM((S, G * rows, lifted), BF16),
            pltpu.VMEM((S, G * rows, lifted), BF16),
            pltpu.VMEM((S, G * rows, lifted), BF16),
            pltpu.VMEM((S, G * rows, lifted), BF16),
            pltpu.VMEM((N, G * rows, lifted), BF16),
            pltpu.VMEM((G * rows, block), F32),
            pltpu.VMEM((G, rows, block), BF16),
            pltpu.VMEM((G, rows, block), BF16),
            dma((11,)),
            dma((N,)),
            dma((N,)),
            dma((N,)),
            dma((N,)),
            dma((N,)),
            dma((N,)),
            dma((N,)),
            dma((N,)),
            dma((G,)),
            dma((G,)),
            dma((S,)),
            dma((S,)),
            dma((S,)),
            dma((S,)),
            dma((S,)),
            dma((S,)),
            dma((N,)),
            dma((G,)),
            dma((G,)),
        ],
        compiler_params=pltpu.CompilerParams(
            collective_id=0, has_side_effects=True, vmem_limit_bytes=44 * 1024 * 1024
        ),
        cost_estimate=pl.CostEstimate(
            flops=2 * rows * width * (keys * 2 + block) + 4 * G * rows * block * w_up.shape[1],
            bytes_accessed=4 * keys * width + 2 * (w_out.size + w_up.size + w_down.size),
            transcendentals=rows * keys * H,
        ),
    )(
        queries,
        new_keys,
        new_values,
        prefix_keys,
        prefix_values,
        tail_keys,
        tail_values,
        prefix_len,
        tail_len,
        slopes,
        resid,
        ln_gain.reshape(1, block),
        w_out,
        w_up,
        w_down,
    )


def layer_body(mesh):
    G, S, C = (mesh.shape[axis] for axis in ("grp", "seq", "mlp"))

    def run(*args):
        rows = args[0].shape[0] * args[0].shape[1]
        block = args[9].shape[2]
        lifted = args[12].shape[1] // (S * C)
        if C == 2 and lifted == block and block % LANES == 0 and rows == NEW_PAD:
            return fused(G, S, C, *args)
        return body(*args)

    return run


def solution(mesh):
    return jax.shard_map(
        layer_body(mesh),
        mesh=mesh,
        in_specs=(
            P("grp", None, None),
            P(("grp", "seq"), None, None),
            P(("grp", "seq"), None, None),
            P("grp", ("seq", "mlp"), None),
            P("grp", ("seq", "mlp"), None),
            P(("grp", "seq"), "mlp", None),
            P(("grp", "seq"), "mlp", None),
            P("grp"),
            P("grp"),
            P("grp", None, ("seq", "mlp")),
            P(None, ("seq", "mlp")),
            P(("seq", "mlp")),
            P(("seq", "mlp"), "grp"),
            P("grp", ("seq", "mlp")),
        ),
        out_specs=P("grp", None, ("seq", "mlp")),
        check_vma=False,
    )
```

```python
import functools
import math

import jax
import jax.numpy as jnp
import numpy as np
from jax import lax
from jax.experimental import pallas as pl
from jax.experimental.pallas import tpu as pltpu
from jax.sharding import PartitionSpec as P

D = 4096
H = 32


NEG = -1e30


def merged(value, axis, join):
    pieces = jax.tree.map(lambda part: lax.all_gather(part, axis), value)
    head = jax.tree.map(lambda part: part[0], pieces)
    tail = jax.tree.map(lambda part: part[1:], pieces)
    so_far, _ = lax.scan(lambda so_far, piece: (join(so_far, piece), None), head, tail)
    return so_far


def head_slopes(count):
    return jnp.power(2.0, -8.0 * (jnp.arange(count, dtype=jnp.float32) + 1.0) / count)


def attend(query_rows, key_block, value_block, query_pos, key_pos, key_mask):
    head_count = query_rows.shape[1]
    inv_scale = 1.0 / math.sqrt(query_rows.shape[2])
    scores = (
        jnp.einsum("qhd,khd->hqk", query_rows, key_block, preferred_element_type=jnp.float32)
        * inv_scale
    )
    distance = (query_pos[:, None] - key_pos[None, :]).astype(jnp.float32)
    scores = scores - head_slopes(head_count)[:, None, None] * distance[None, :, :]
    scores = jnp.where(key_mask, scores, NEG)
    row_max = jnp.max(scores, axis=2)
    weights = jnp.where(key_mask, jnp.exp(scores - row_max[:, :, None]), 0.0)
    weight_sum = jnp.sum(weights, axis=2)
    mixed_sum = jnp.einsum(
        "hqk,khd->qhd",
        weights.astype(jnp.bfloat16),
        value_block,
        preferred_element_type=jnp.float32,
    )
    return (row_max.T, weight_sum.T, mixed_sum)


def join_parts(first, second):
    best_max = jnp.maximum(first[0], second[0])
    factor_one = jnp.exp(first[0] - best_max)
    factor_two = jnp.exp(second[0] - best_max)
    return (
        best_max,
        first[1] * factor_one + second[1] * factor_two,
        first[2] * factor_one[:, :, None] + second[2] * factor_two[:, :, None],
    )


def body(
    queries,
    new_keys,
    new_values,
    prefix_keys,
    prefix_values,
    tail_keys,
    tail_values,
    prefix_len,
    tail_len,
    resid,
    w_out,
    ln_gain,
    w_up,
    w_down,
):
    group_req, step_count, model_width = queries.shape
    head_dim = model_width // H
    row_count = group_req * step_count
    seq_index = lax.axis_index("seq")
    core_index = lax.axis_index("mlp")
    block_len = prefix_keys.shape[1]
    tail_block = tail_keys.shape[1]
    block_start = (seq_index * lax.axis_size("mlp") + core_index) * block_len
    prefix_end = prefix_len[0]
    step_index = jnp.arange(step_count, dtype=jnp.int32)
    query_pos = prefix_end + jnp.repeat(tail_len, step_count) + jnp.tile(step_index, group_req)
    query_rows = queries.reshape(row_count, H, head_dim)
    key_pos = block_start + jnp.arange(block_len, dtype=jnp.int32)
    key_live = key_pos < prefix_end
    own_len = lax.dynamic_index_in_dim(tail_len, seq_index, 0, keepdims=False)
    own_rows = lax.dynamic_slice_in_dim(query_rows, seq_index * step_count, step_count, 0)
    own_pos = prefix_end + own_len + step_index
    tail_index = core_index * tail_block + jnp.arange(tail_block, dtype=jnp.int32)
    partial_value = attend(
        query_rows,
        prefix_keys[0].reshape(block_len, H, head_dim),
        prefix_values[0].reshape(block_len, H, head_dim),
        query_pos,
        key_pos,
        key_live[None, None, :],
    )
    tail_result = attend(
        own_rows,
        tail_keys[0].reshape(tail_block, H, head_dim),
        tail_values[0].reshape(tail_block, H, head_dim),
        own_pos,
        prefix_end + tail_index,
        (tail_index < own_len)[None, None, :],
    )
    self_mask = (step_index[None, :] <= step_index[:, None]) & (core_index == 0)
    self_result = attend(
        own_rows,
        new_keys[0].reshape(step_count, H, head_dim),
        new_values[0].reshape(step_count, H, head_dim),
        own_pos,
        own_pos,
        self_mask[None, :, :],
    )
    own_slice = tuple(
        (
            lax.dynamic_slice_in_dim(member, seq_index * step_count, step_count, 0)
            for member in partial_value
        )
    )
    own_part = join_parts(join_parts(own_slice, tail_result), self_result)
    partial_value = tuple(
        (
            lax.dynamic_update_slice_in_dim(member, update, seq_index * step_count, 0)
            for member, update in zip(partial_value, own_part)
        )
    )
    row_max, weight_sum, mixed_sum = merged(
        (partial_value[0], partial_value[1], partial_value[2]), ("seq", "mlp"), join_parts
    )
    attention = (
        (mixed_sum / weight_sum[:, :, None]).astype(jnp.bfloat16).reshape(row_count, model_width)
    )
    width_block = resid.shape[2]
    stream = resid.astype(jnp.float32).reshape(row_count, width_block) + jnp.dot(
        attention, w_out, preferred_element_type=jnp.float32
    )
    row_sums, squares = lax.psum(
        (jnp.sum(stream, axis=1), jnp.sum(stream * stream, axis=1)), ("seq", "mlp")
    )
    row_mean = row_sums / D
    row_var = squares / D - row_mean * row_mean
    hidden = (
        (stream - row_mean[:, None])
        * lax.rsqrt(row_var[:, None] + 1e-05)
        * ln_gain.astype(jnp.float32)
    ).astype(jnp.bfloat16)
    lifted = jnp.dot(
        lax.all_gather(hidden, "grp", axis=0, tiled=True), w_up, preferred_element_type=jnp.float32
    )
    summed = lax.psum(lifted, ("seq", "mlp"))
    activated = jax.nn.gelu(summed, approximate=False).astype(jnp.bfloat16)
    projected = lax.psum_scatter(
        jnp.dot(activated, w_down, preferred_element_type=jnp.float32),
        "grp",
        scatter_dimension=0,
        tiled=True,
    )
    return (stream + projected).reshape(group_req, step_count, width_block)


F32 = jnp.float32
BF16 = jnp.bfloat16
LANES = 128
NEW_PAD = 16
FLOOR = -1e29
FAR = 1e33


def remote(src, dst, send_sem, recv_sem, device):
    return pltpu.make_async_remote_copy(
        src_ref=src,
        dst_ref=dst,
        send_sem=send_sem,
        recv_sem=recv_sem,
        device_id=device,
        device_id_type=pl.DeviceIdType.MESH,
    )


def layer_kernel(
    G,
    S,
    C,
    q_hbm,
    nk_hbm,
    nv_hbm,
    pk_hbm,
    pv_hbm,
    tk_hbm,
    tv_hbm,
    plen,
    tlen,
    slopes,
    resid_hbm,
    gain_ref,
    wo_hbm,
    wu_hbm,
    wd_hbm,
    out_ref,
    q_in,
    nk_in,
    nv_in,
    resid_in,
    stage,
    qbuf,
    kbuf,
    vbuf,
    dist,
    wo,
    wu,
    wd,
    o_send,
    o_recv,
    st_send,
    st_recv,
    att,
    ybuf,
    sum_send,
    sum_recv,
    hid,
    up_send,
    up_pair,
    up_zsend,
    up_zrecv,
    act,
    acc,
    proj_send,
    proj_recv,
    load_sem,
    cache_sem,
    o_ss,
    o_rs,
    st_ss,
    st_rs,
    att_ss,
    att_rs,
    sum_ss,
    sum_rs,
    hid_ss,
    hid_rs,
    pair_ss,
    pair_rs,
    zup_ss,
    zup_rs,
    act_ss,
    fwd_ss,
    act_rs,
    proj_ss,
    proj_rs,
):
    N = S * C
    grp = lax.axis_index("grp")
    seq = lax.axis_index("seq")
    core = lax.axis_index("mlp")
    me = seq * C + core
    group_req, steps, width = q_in.shape
    rows = group_req * steps
    prefix = pk_hbm.shape[1]
    tail = tk_hbm.shape[1]
    keys = kbuf.shape[0]
    block = ybuf.shape[1]
    head_dim = width // H
    heads = block // head_dim

    def peer(index):
        return {"seq": index // C, "mlp": lax.rem(index, C)}

    def across(k):
        return 2 * lax.rem(seq // 2 + k // 2, 2) + lax.rem(lax.rem(seq, 2) + lax.rem(k, 2), 2)

    def partner(k):
        return across(k // 2) * C + lax.rem(core + lax.rem(k, 2), 2)

    small = [
        pltpu.make_async_copy(q_hbm, q_in, load_sem.at[0]),
        pltpu.make_async_copy(nk_hbm, nk_in, load_sem.at[1]),
        pltpu.make_async_copy(nv_hbm, nv_in, load_sem.at[2]),
        pltpu.make_async_copy(resid_hbm, resid_in, load_sem.at[3]),
    ]

    def cache_loads(k):
        cols = pl.ds(pl.multiple_of(partner(k) * block, block), block)
        first, second = pl.ds(0, prefix), pl.ds(prefix, tail)
        return [
            pltpu.make_async_copy(pk_hbm.at[0, :, cols], kbuf.at[first, cols], cache_sem.at[0, k]),
            pltpu.make_async_copy(tk_hbm.at[0, :, cols], kbuf.at[second, cols], cache_sem.at[1, k]),
            pltpu.make_async_copy(pv_hbm.at[0, :, cols], vbuf.at[first, cols], cache_sem.at[2, k]),
            pltpu.make_async_copy(tv_hbm.at[0, :, cols], vbuf.at[second, cols], cache_sem.at[3, k]),
        ]

    wo_load = pltpu.make_async_copy(wo_hbm, wo, load_sem.at[4])
    wu_load = pltpu.make_async_copy(wu_hbm, wu, load_sem.at[5])
    wd_load = pltpu.make_async_copy(wd_hbm, wd, load_sem.at[6])
    for load in small:
        load.start()

    def start_cache(i, carry):
        for load in cache_loads(N - 1 - i):
            load.start()
        return carry

    lax.fori_loop(0, N, start_cache, 0)

    barrier = pltpu.get_barrier_semaphore()
    for k in range(1, N):
        pl.semaphore_signal(
            barrier, inc=1, device_id=peer(lax.rem(me + k, N)), device_id_type=pl.DeviceIdType.MESH
        )
    for k in range(1, G):
        pl.semaphore_signal(
            barrier,
            inc=1,
            device_id={"grp": lax.rem(grp + k, G)},
            device_id_type=pl.DeviceIdType.MESH,
        )

    row = lax.broadcasted_iota(jnp.int32, (rows, keys), 0)
    col = lax.broadcasted_iota(jnp.int32, (rows, keys), 1)
    request = row // steps
    step = row - request * steps
    prefix_end = plen[0]
    length = jnp.zeros((rows, keys), jnp.int32)
    for r in range(group_req):
        length = jnp.where(request == r, tlen[r], length)
    own = request == seq
    key_pos = me * prefix + col
    tail_pos = core * tail + col - prefix
    new_pos = col - prefix - tail
    is_prefix = col < prefix
    is_tail = jnp.logical_and(col >= prefix, col < prefix + tail)
    is_new = jnp.logical_and(col >= prefix + tail, new_pos < steps)
    apart = jnp.where(
        is_prefix,
        prefix_end + length + step - key_pos,
        jnp.where(is_tail, length + step - tail_pos, step - new_pos),
    )
    live_prefix = jnp.logical_and(is_prefix, key_pos < prefix_end)
    live_tail = jnp.logical_and(jnp.logical_and(is_tail, tail_pos < length), own)
    live_new = jnp.logical_and(
        jnp.logical_and(is_new, new_pos <= step), jnp.logical_and(own, core == 0)
    )
    live = jnp.logical_or(live_prefix, jnp.logical_or(live_tail, live_new))
    dist[...] = jnp.where(live, apart.astype(F32), FAR)

    stage[...] = jnp.zeros_like(stage)
    small[1].wait()
    stage[0:steps, :] = nk_in[0].astype(F32)
    kbuf[prefix + tail : keys, :] = stage[...].astype(BF16)
    small[2].wait()
    stage[0:steps, :] = nv_in[0].astype(F32)
    vbuf[prefix + tail : keys, :] = stage[...].astype(BF16)
    small[0].wait()
    for r in range(group_req):
        stage[r * steps : (r + 1) * steps, :] = q_in[r].astype(F32)
    qbuf[...] = stage[...].astype(BF16)
    small[3].wait()
    for r in range(group_req):
        ybuf[r * steps : (r + 1) * steps, :] = resid_in[r].astype(F32)

    wo_load.start()
    wu_load.start()
    wd_load.start()

    pl.semaphore_wait(barrier, N - 1 + G - 1)

    inv_scale = 1.0 / math.sqrt(head_dim)
    lane = lax.broadcasted_iota(jnp.int32, (rows, LANES), 1)

    def partials(i, carry):
        pair = [N - 1 - 2 * i, N - 2 - 2 * i]
        for k in pair:
            for load in cache_loads(k):
                load.wait()
        places = [(partner(k), j) for k in pair for j in range(heads)]
        spans = [
            pl.ds(pl.multiple_of(p * block, block) + j * head_dim, head_dim) for p, j in places
        ]
        scores = [
            lax.dot_general(
                qbuf[:, cols], kbuf[:, cols], (((1,), (1,)), ((), ())), preferred_element_type=F32
            )
            for cols in spans
        ]
        scores = [
            member * inv_scale - slopes[p * heads + j] * dist[...]
            for member, (p, j) in zip(scores, places)
        ]
        tops = [
            jnp.maximum(jnp.max(member, axis=1, keepdims=True), FLOOR) for member in scores
        ]
        weights = [jnp.exp(member - top) for member, top in zip(scores, tops)]
        totals = [jnp.sum(member, axis=1, keepdims=True) for member in weights]
        mixed = [
            jnp.dot(member.astype(BF16), vbuf[:, cols], preferred_element_type=F32)
            for member, cols in zip(weights, spans)
        ]
        for half in range(2):
            p = places[half * heads][0]
            stats = jnp.zeros((rows, LANES), F32)
            for j in range(heads):
                at = half * heads + j
                o_send[p, :, j * head_dim : (j + 1) * head_dim] = mixed[at].astype(BF16)
                stats = jnp.where(lane == j, tops[at], stats)
                stats = jnp.where(lane == heads + j, totals[at], stats)
            st_send[p] = stats

            @pl.when(pair[half] > 0)
            def _():
                remote(o_send.at[p], o_recv.at[me], o_ss.at[p], o_rs.at[me], peer(p)).start()
                remote(st_send.at[p], st_recv.at[me], st_ss.at[p], st_rs.at[me], peer(p)).start()

        return carry

    lax.fori_loop(0, N // 2, partials, 0)
    o_recv[me] = o_send[me]
    st_recv[me] = st_send[me]

    for k in range(1, N):
        p = lax.rem(me + N - k, N)
        remote(o_send.at[p], o_recv.at[p], o_ss.at[p], o_rs.at[p], peer(p)).wait_recv()
        remote(st_send.at[p], st_recv.at[p], st_ss.at[p], st_rs.at[p], peer(p)).wait_recv()
    stats = [st_recv[i] for i in range(N)]
    best = stats[0]
    for i in range(1, N):
        best = jnp.maximum(best, stats[i])
    factors = [jnp.exp(member - best) for member in stats]
    whole = factors[0] * pltpu.roll(stats[0], LANES - heads, 1)
    for i in range(1, N):
        whole = whole + factors[i] * pltpu.roll(stats[i], LANES - heads, 1)
    for j in range(heads):
        cols = slice(j * head_dim, (j + 1) * head_dim)
        mixed = o_recv[0, :, cols].astype(F32) * factors[0][:, j : j + 1]
        for i in range(1, N):
            mixed = mixed + o_recv[i, :, cols].astype(F32) * factors[i][:, j : j + 1]
        att[me, :, cols] = (mixed / whole[:, j : j + 1]).astype(BF16)
    for k in range(N - 1, 0, -1):
        p = partner(k)
        remote(att.at[me], att.at[me], att_ss.at[p], att_rs.at[me], peer(p)).start()

    wo_load.wait()

    def out_proj(k, carry):
        p = partner(k)

        @pl.when(k > 0)
        def _():
            remote(att.at[p], att.at[p], att_ss.at[p], att_rs.at[p], peer(p)).wait_recv()

        piece = pl.ds(pl.multiple_of(p * block, block), block)
        ybuf[...] += jnp.dot(att[p], wo[piece, :], preferred_element_type=F32)
        return carry

    lax.fori_loop(0, N, out_proj, 0)

    y = ybuf[...]
    sums = jnp.where(lane == 0, jnp.sum(y, axis=1, keepdims=True), 0.0)
    sums = jnp.where(lane == 1, jnp.sum(y * y, axis=1, keepdims=True), sums)
    sum_send[...] = sums
    for k in range(N - 1, 0, -1):
        p = partner(k)
        remote(sum_send, sum_recv.at[me], sum_ss.at[p], sum_rs.at[me], peer(p)).start()
    sum_recv[me] = sums
    for k in range(1, N):
        p = lax.rem(me + N - k, N)
        remote(sum_send, sum_recv.at[p], sum_ss.at[p], sum_rs.at[p], peer(p)).wait_recv()
    sums = jnp.sum(sum_recv[...], axis=0)
    mean = sums[:, 0:1] / width
    var = sums[:, 1:2] / width - mean * mean
    hidden = (y - mean) * lax.rsqrt(var + 1e-05) * gain_ref[...].astype(F32)[None, :]
    mine = pl.ds(pl.multiple_of(grp * rows, rows), rows)
    hid[mine, :] = hidden.astype(BF16)
    for k in range(1, G):
        g = lax.rem(grp + k, G)
        remote(hid.at[mine], hid.at[mine], hid_ss.at[g], hid_rs.at[grp], {"grp": g}).start()
    wu_load.wait()
    for k in range(1, G):
        g = lax.rem(grp + G - k, G)
        theirs = pl.ds(pl.multiple_of(g * rows, rows), rows)
        remote(hid.at[theirs], hid.at[theirs], hid_ss.at[g], hid_rs.at[g], {"grp": g}).wait_recv()

    other = 1 - core

    def lift(index):
        piece = pl.ds(pl.multiple_of(index * act.shape[2], act.shape[2]), act.shape[2])
        return jnp.dot(hid[...], wu[:, piece], preferred_element_type=F32)

    def pair_blocks(k, carry):
        z = across(S - 1 - k)
        up_send[z] = lift(z * C + other).astype(BF16)
        remote(up_send.at[z], up_pair.at[z], pair_ss.at[z], pair_rs.at[z], {"mlp": other}).start()
        return carry

    lax.fori_loop(0, S, pair_blocks, 0)

    def z_blocks(k, carry):
        z = across(S - 1 - k)
        part = lift(z * C + core)
        remote(
            up_send.at[z], up_pair.at[z], pair_ss.at[z], pair_rs.at[z], {"mlp": other}
        ).wait_recv()
        part = part + up_pair[z].astype(F32)

        @pl.when(k < S - 1)
        def _():
            up_zsend[z] = part.astype(BF16)
            remote(
                up_zsend.at[z], up_zrecv.at[seq], zup_ss.at[z], zup_rs.at[seq], {"seq": z}
            ).start()

        @pl.when(k == S - 1)
        def _():
            acc[...] = part

        return carry

    lax.fori_loop(0, S, z_blocks, 0)
    lifted = acc[...]
    for k in range(1, S):
        z = lax.rem(seq + S - k, S)
        remote(
            up_zsend.at[z], up_zrecv.at[z], zup_ss.at[z], zup_rs.at[z], {"seq": z}
        ).wait_recv()
        lifted = lifted + up_zrecv[z].astype(F32)
    act[me] = (0.5 * lifted * (1.0 + lax.erf(lifted * math.sqrt(0.5)))).astype(BF16)

    for k in range(S - 1, 0, -1):
        z = across(k)
        remote(act.at[me], act.at[me], act_ss.at[z], act_rs.at[me], {"seq": z}).start()
    remote(act.at[me], act.at[me], fwd_ss.at[seq], act_rs.at[me], {"mlp": other}).start()

    wd_load.wait()

    def lower(index):
        piece = pl.ds(pl.multiple_of(index * act.shape[2], act.shape[2]), act.shape[2])
        return jnp.dot(act[index], wd[piece, :], preferred_element_type=F32)

    acc[...] = lower(me)

    def down(k, carry):
        z = across(k)
        near = z * C + core
        far = z * C + other

        @pl.when(k > 0)
        def _():
            remote(act.at[near], act.at[near], act_ss.at[z], act_rs.at[near], {"seq": z}).wait_recv()
            remote(act.at[near], act.at[near], fwd_ss.at[z], act_rs.at[near], {"mlp": other}).start()
            acc[...] += lower(near)

        remote(act.at[far], act.at[far], fwd_ss.at[z], act_rs.at[far], {"mlp": other}).wait_recv()
        acc[...] += lower(far)
        return carry

    lax.fori_loop(0, S, down, 0)

    for k in range(1, G):
        g = lax.rem(grp + k, G)
        theirs = pl.ds(pl.multiple_of(g * rows, rows), rows)
        proj_send[g] = acc[theirs, :].astype(BF16)
        remote(
            proj_send.at[g], proj_recv.at[grp], proj_ss.at[g], proj_rs.at[grp], {"grp": g}
        ).start()
    total = ybuf[...] + acc[mine, :]
    for k in range(1, G):
        g = lax.rem(grp + G - k, G)
        remote(
            proj_send.at[g], proj_recv.at[g], proj_ss.at[g], proj_rs.at[g], {"grp": g}
        ).wait_recv()
        total = total + proj_recv[g].astype(F32)
    ybuf[...] = total
    for r in range(group_req):
        out_ref[r] = ybuf[r * steps : (r + 1) * steps, :]

    for k in range(1, N):
        p = lax.rem(me + k, N)
        remote(o_send.at[p], o_recv.at[me], o_ss.at[p], o_rs.at[me], peer(p)).wait_send()
        remote(st_send.at[p], st_recv.at[me], st_ss.at[p], st_rs.at[me], peer(p)).wait_send()
        remote(att.at[me], att.at[me], att_ss.at[p], att_rs.at[me], peer(p)).wait_send()
        remote(sum_send, sum_recv.at[me], sum_ss.at[p], sum_rs.at[me], peer(p)).wait_send()
    for k in range(1, G):
        g = lax.rem(grp + k, G)
        remote(hid.at[mine], hid.at[mine], hid_ss.at[g], hid_rs.at[grp], {"grp": g}).wait_send()
        remote(
            proj_send.at[g], proj_recv.at[grp], proj_ss.at[g], proj_rs.at[grp], {"grp": g}
        ).wait_send()
    for z in range(S):
        remote(
            up_send.at[z], up_pair.at[z], pair_ss.at[z], pair_rs.at[z], {"mlp": other}
        ).wait_send()
        near = z * C + core
        remote(act.at[near], act.at[near], fwd_ss.at[z], act_rs.at[near], {"mlp": other}).wait_send()
    for k in range(1, S):
        z = lax.rem(seq + k, S)
        remote(
            up_zsend.at[z], up_zrecv.at[seq], zup_ss.at[z], zup_rs.at[seq], {"seq": z}
        ).wait_send()
        remote(act.at[me], act.at[me], act_ss.at[z], act_rs.at[me], {"seq": z}).wait_send()


def fused(
    G,
    S,
    C,
    queries,
    new_keys,
    new_values,
    prefix_keys,
    prefix_values,
    tail_keys,
    tail_values,
    prefix_len,
    tail_len,
    resid,
    w_out,
    ln_gain,
    w_up,
    w_down,
):
    group_req, steps, width = queries.shape
    rows = group_req * steps
    N = S * C
    block = resid.shape[2]
    lifted = w_up.shape[1] // N
    keys = prefix_keys.shape[1] + tail_keys.shape[1] + NEW_PAD
    slopes = jnp.asarray(np.power(2.0, -8.0 * (np.arange(H) + 1.0) / H).astype(np.float32))
    dma = pltpu.SemaphoreType.DMA
    hbm = pl.BlockSpec(memory_space=pl.ANY)
    smem = pl.BlockSpec(memory_space=pltpu.SMEM)
    vmem = pl.BlockSpec(memory_space=pltpu.VMEM)
    return pl.pallas_call(
        functools.partial(layer_kernel, G, S, C),
        out_shape=jax.ShapeDtypeStruct((group_req, steps, block), F32),
        in_specs=[hbm] * 7 + [smem] * 3 + [hbm, vmem] + [hbm] * 3,
        out_specs=vmem,
        scratch_shapes=[
            pltpu.VMEM(queries.shape, BF16),
            pltpu.VMEM(new_keys.shape, BF16),
            pltpu.VMEM(new_values.shape, BF16),
            pltpu.VMEM(resid.shape, BF16),
            pltpu.VMEM((rows, width), F32),
            pltpu.VMEM((rows, width), BF16),
            pltpu.VMEM((keys, width), BF16),
            pltpu.VMEM((keys, width), BF16),
            pltpu.VMEM((rows, keys), F32),
            pltpu.VMEM(w_out.shape, BF16),
            pltpu.VMEM(w_up.shape, BF16),
            pltpu.VMEM(w_down.shape, BF16),
            pltpu.VMEM((N, rows, block), BF16),
            pltpu.VMEM((N, rows, block), BF16),
            pltpu.VMEM((N, rows, LANES), F32),
            pltpu.VMEM((N, rows, LANES), F32),
            pltpu.VMEM((N, rows, block), BF16),
            pltpu.VMEM((rows, block), F32),
            pltpu.VMEM((rows, LANES), F32),
            pltpu.VMEM((N, rows, LANES), F32),
            pltpu.VMEM((G * rows, block), BF16),
            pltpu.VMEM((S, G * rows, lifted), BF16),
            pltpu.VMEM((S, G * rows, lifted), BF16),
            pltpu.VMEM((S, G * rows, lifted), BF16),
            pltpu.VMEM((S, G * rows, lifted), BF16),
            pltpu.VMEM((N, G * rows, lifted), BF16),
            pltpu.VMEM((G * rows, block), F32),
            pltpu.VMEM((G, rows, block), BF16),
            pltpu.VMEM((G, rows, block), BF16),
            dma((7,)),
            dma((4, N)),
            dma((N,)),
            dma((N,)),
            dma((N,)),
            dma((N,)),
            dma((N,)),
            dma((N,)),
            dma((N,)),
            dma((N,)),
            dma((G,)),
            dma((G,)),
            dma((S,)),
            dma((S,)),
            dma((S,)),
            dma((S,)),
            dma((S,)),
            dma((S,)),
            dma((N,)),
            dma((G,)),
            dma((G,)),
        ],
        compiler_params=pltpu.CompilerParams(
            collective_id=0, has_side_effects=True, vmem_limit_bytes=63 * 1024 * 1024
        ),
        cost_estimate=pl.CostEstimate(
            flops=2 * rows * width * (keys * 2 + block) + 4 * G * rows * block * w_up.shape[1],
            bytes_accessed=4 * keys * width + 2 * (w_out.size + w_up.size + w_down.size),
            transcendentals=rows * keys * H,
        ),
    )(
        queries,
        new_keys,
        new_values,
        prefix_keys,
        prefix_values,
        tail_keys,
        tail_values,
        prefix_len,
        tail_len,
        slopes,
        resid,
        ln_gain,
        w_out,
        w_up,
        w_down,
    )


def layer_body(mesh):
    G, S, C = (mesh.shape[axis] for axis in ("grp", "seq", "mlp"))

    def run(*args):
        rows = args[0].shape[0] * args[0].shape[1]
        block = args[9].shape[2]
        lifted = args[12].shape[1] // (S * C)
        if (S, C) == (4, 2) and lifted == block and block % LANES == 0 and rows == NEW_PAD:
            return fused(G, S, C, *args)
        return body(*args)

    return run


def solution(mesh):
    return jax.shard_map(
        layer_body(mesh),
        mesh=mesh,
        in_specs=(
            P("grp", None, None),
            P(("grp", "seq"), None, None),
            P(("grp", "seq"), None, None),
            P("grp", ("seq", "mlp"), None),
            P("grp", ("seq", "mlp"), None),
            P(("grp", "seq"), "mlp", None),
            P(("grp", "seq"), "mlp", None),
            P("grp"),
            P("grp"),
            P("grp", None, ("seq", "mlp")),
            P(None, ("seq", "mlp")),
            P(("seq", "mlp")),
            P(("seq", "mlp"), "grp"),
            P("grp", ("seq", "mlp")),
        ),
        out_specs=P("grp", None, ("seq", "mlp")),
        check_vma=False,
    )
```

```python
import functools
import math

import jax
import jax.numpy as jnp
import numpy as np
from jax import lax
from jax.experimental import pallas as pl
from jax.experimental.pallas import tpu as pltpu
from jax.sharding import PartitionSpec as P

D = 4096
H = 32


NEG = -1e30


def merged(value, axis, join):
    pieces = jax.tree.map(lambda part: lax.all_gather(part, axis), value)
    head = jax.tree.map(lambda part: part[0], pieces)
    tail = jax.tree.map(lambda part: part[1:], pieces)
    so_far, _ = lax.scan(lambda so_far, piece: (join(so_far, piece), None), head, tail)
    return so_far


def head_slopes(count):
    return jnp.power(2.0, -8.0 * (jnp.arange(count, dtype=jnp.float32) + 1.0) / count)


def attend(query_rows, key_block, value_block, query_pos, key_pos, key_mask):
    head_count = query_rows.shape[1]
    inv_scale = 1.0 / math.sqrt(query_rows.shape[2])
    scores = (
        jnp.einsum("qhd,khd->hqk", query_rows, key_block, preferred_element_type=jnp.float32)
        * inv_scale
    )
    distance = (query_pos[:, None] - key_pos[None, :]).astype(jnp.float32)
    scores = scores - head_slopes(head_count)[:, None, None] * distance[None, :, :]
    scores = jnp.where(key_mask, scores, NEG)
    row_max = jnp.max(scores, axis=2)
    weights = jnp.where(key_mask, jnp.exp(scores - row_max[:, :, None]), 0.0)
    weight_sum = jnp.sum(weights, axis=2)
    mixed_sum = jnp.einsum(
        "hqk,khd->qhd",
        weights.astype(jnp.bfloat16),
        value_block,
        preferred_element_type=jnp.float32,
    )
    return (row_max.T, weight_sum.T, mixed_sum)


def join_parts(first, second):
    best_max = jnp.maximum(first[0], second[0])
    factor_one = jnp.exp(first[0] - best_max)
    factor_two = jnp.exp(second[0] - best_max)
    return (
        best_max,
        first[1] * factor_one + second[1] * factor_two,
        first[2] * factor_one[:, :, None] + second[2] * factor_two[:, :, None],
    )


def body(
    queries,
    new_keys,
    new_values,
    prefix_keys,
    prefix_values,
    tail_keys,
    tail_values,
    prefix_len,
    tail_len,
    resid,
    w_out,
    ln_gain,
    w_up,
    w_down,
):
    group_req, step_count, model_width = queries.shape
    head_dim = model_width // H
    row_count = group_req * step_count
    seq_index = lax.axis_index("seq")
    core_index = lax.axis_index("mlp")
    block_len = prefix_keys.shape[1]
    tail_block = tail_keys.shape[1]
    block_start = (seq_index * lax.axis_size("mlp") + core_index) * block_len
    prefix_end = prefix_len[0]
    step_index = jnp.arange(step_count, dtype=jnp.int32)
    query_pos = prefix_end + jnp.repeat(tail_len, step_count) + jnp.tile(step_index, group_req)
    query_rows = queries.reshape(row_count, H, head_dim)
    key_pos = block_start + jnp.arange(block_len, dtype=jnp.int32)
    key_live = key_pos < prefix_end
    own_len = lax.dynamic_index_in_dim(tail_len, seq_index, 0, keepdims=False)
    own_rows = lax.dynamic_slice_in_dim(query_rows, seq_index * step_count, step_count, 0)
    own_pos = prefix_end + own_len + step_index
    tail_index = core_index * tail_block + jnp.arange(tail_block, dtype=jnp.int32)
    partial_value = attend(
        query_rows,
        prefix_keys[0].reshape(block_len, H, head_dim),
        prefix_values[0].reshape(block_len, H, head_dim),
        query_pos,
        key_pos,
        key_live[None, None, :],
    )
    tail_result = attend(
        own_rows,
        tail_keys[0].reshape(tail_block, H, head_dim),
        tail_values[0].reshape(tail_block, H, head_dim),
        own_pos,
        prefix_end + tail_index,
        (tail_index < own_len)[None, None, :],
    )
    self_mask = (step_index[None, :] <= step_index[:, None]) & (core_index == 0)
    self_result = attend(
        own_rows,
        new_keys[0].reshape(step_count, H, head_dim),
        new_values[0].reshape(step_count, H, head_dim),
        own_pos,
        own_pos,
        self_mask[None, :, :],
    )
    own_slice = tuple(
        (
            lax.dynamic_slice_in_dim(member, seq_index * step_count, step_count, 0)
            for member in partial_value
        )
    )
    own_part = join_parts(join_parts(own_slice, tail_result), self_result)
    partial_value = tuple(
        (
            lax.dynamic_update_slice_in_dim(member, update, seq_index * step_count, 0)
            for member, update in zip(partial_value, own_part)
        )
    )
    row_max, weight_sum, mixed_sum = merged(
        (partial_value[0], partial_value[1], partial_value[2]), ("seq", "mlp"), join_parts
    )
    attention = (
        (mixed_sum / weight_sum[:, :, None]).astype(jnp.bfloat16).reshape(row_count, model_width)
    )
    width_block = resid.shape[2]
    stream = resid.astype(jnp.float32).reshape(row_count, width_block) + jnp.dot(
        attention, w_out, preferred_element_type=jnp.float32
    )
    row_sums, squares = lax.psum(
        (jnp.sum(stream, axis=1), jnp.sum(stream * stream, axis=1)), ("seq", "mlp")
    )
    row_mean = row_sums / D
    row_var = squares / D - row_mean * row_mean
    hidden = (
        (stream - row_mean[:, None])
        * lax.rsqrt(row_var[:, None] + 1e-05)
        * ln_gain.astype(jnp.float32)
    ).astype(jnp.bfloat16)
    lifted = jnp.dot(
        lax.all_gather(hidden, "grp", axis=0, tiled=True), w_up, preferred_element_type=jnp.float32
    )
    summed = lax.psum(lifted, ("seq", "mlp"))
    activated = jax.nn.gelu(summed, approximate=False).astype(jnp.bfloat16)
    projected = lax.psum_scatter(
        jnp.dot(activated, w_down, preferred_element_type=jnp.float32),
        "grp",
        scatter_dimension=0,
        tiled=True,
    )
    return (stream + projected).reshape(group_req, step_count, width_block)


F32 = jnp.float32
BF16 = jnp.bfloat16
LANES = 128
NEW_PAD = 16
FLOOR = -1e29
FAR = 1e33


def remote(src, dst, send_sem, recv_sem, device):
    return pltpu.make_async_remote_copy(
        src_ref=src,
        dst_ref=dst,
        send_sem=send_sem,
        recv_sem=recv_sem,
        device_id=device,
        device_id_type=pl.DeviceIdType.MESH,
    )


def layer_kernel(
    G,
    S,
    C,
    q_hbm,
    nk_hbm,
    nv_hbm,
    pk_hbm,
    pv_hbm,
    tk_hbm,
    tv_hbm,
    plen,
    tlen,
    slopes,
    resid_hbm,
    gain_ref,
    wo_hbm,
    wu_hbm,
    wd_hbm,
    out_ref,
    q_in,
    nk_in,
    nv_in,
    resid_in,
    stage,
    qbuf,
    kbuf,
    vbuf,
    dist,
    wo,
    wu,
    wd,
    o_send,
    o_recv,
    st_send,
    st_recv,
    att,
    ybuf,
    sum_send,
    sum_recv,
    hid,
    up_send,
    up_pair,
    up_zsend,
    up_zrecv,
    act,
    acc,
    proj_send,
    proj_recv,
    load_sem,
    cache_sem,
    o_ss,
    o_rs,
    st_ss,
    st_rs,
    att_ss,
    att_rs,
    sum_ss,
    sum_rs,
    hid_ss,
    hid_rs,
    pair_ss,
    pair_rs,
    zup_ss,
    zup_rs,
    act_ss,
    fwd_ss,
    act_rs,
    proj_ss,
    proj_rs,
):
    N = S * C
    grp = lax.axis_index("grp")
    seq = lax.axis_index("seq")
    core = lax.axis_index("mlp")
    me = seq * C + core
    group_req, steps, width = q_in.shape
    rows = group_req * steps
    prefix = pk_hbm.shape[1]
    tail = tk_hbm.shape[1]
    keys = kbuf.shape[0]
    block = ybuf.shape[1]
    head_dim = width // H
    heads = block // head_dim

    def peer(index):
        return {"seq": index // C, "mlp": lax.rem(index, C)}

    def across(k):
        return 2 * lax.rem(seq // 2 + k // 2, 2) + lax.rem(lax.rem(seq, 2) + lax.rem(k, 2), 2)

    def partner(k):
        return across(k // 2) * C + lax.rem(core + lax.rem(k, 2), 2)

    small = [
        pltpu.make_async_copy(q_hbm, q_in, load_sem.at[0]),
        pltpu.make_async_copy(nk_hbm, nk_in, load_sem.at[1]),
        pltpu.make_async_copy(nv_hbm, nv_in, load_sem.at[2]),
        pltpu.make_async_copy(resid_hbm, resid_in, load_sem.at[3]),
    ]

    def cache_loads(k):
        cols = pl.ds(pl.multiple_of(partner(k) * block, block), block)
        first, second = pl.ds(0, prefix), pl.ds(prefix, tail)
        return [
            pltpu.make_async_copy(pk_hbm.at[0, :, cols], kbuf.at[first, cols], cache_sem.at[0, k]),
            pltpu.make_async_copy(tk_hbm.at[0, :, cols], kbuf.at[second, cols], cache_sem.at[1, k]),
            pltpu.make_async_copy(pv_hbm.at[0, :, cols], vbuf.at[first, cols], cache_sem.at[2, k]),
            pltpu.make_async_copy(tv_hbm.at[0, :, cols], vbuf.at[second, cols], cache_sem.at[3, k]),
        ]

    wo_load = pltpu.make_async_copy(wo_hbm, wo, load_sem.at[4])
    wu_load = pltpu.make_async_copy(wu_hbm, wu, load_sem.at[5])
    wd_load = pltpu.make_async_copy(wd_hbm, wd, load_sem.at[6])
    for load in small:
        load.start()

    def start_cache(i, carry):
        for load in cache_loads(N - 1 - i):
            load.start()
        return carry

    lax.fori_loop(0, N, start_cache, 0)

    barrier = pltpu.get_barrier_semaphore()
    for k in range(1, N):
        pl.semaphore_signal(
            barrier, inc=1, device_id=peer(lax.rem(me + k, N)), device_id_type=pl.DeviceIdType.MESH
        )
    for k in range(1, G):
        pl.semaphore_signal(
            barrier,
            inc=1,
            device_id={"grp": lax.rem(grp + k, G)},
            device_id_type=pl.DeviceIdType.MESH,
        )

    row = lax.broadcasted_iota(jnp.int32, (rows, keys), 0)
    col = lax.broadcasted_iota(jnp.int32, (rows, keys), 1)
    request = row // steps
    step = row - request * steps
    prefix_end = plen[0]
    length = jnp.zeros((rows, keys), jnp.int32)
    for r in range(group_req):
        length = jnp.where(request == r, tlen[r], length)
    own = request == seq
    key_pos = me * prefix + col
    tail_pos = core * tail + col - prefix
    new_pos = col - prefix - tail
    is_prefix = col < prefix
    is_tail = jnp.logical_and(col >= prefix, col < prefix + tail)
    is_new = jnp.logical_and(col >= prefix + tail, new_pos < steps)
    apart = jnp.where(
        is_prefix,
        prefix_end + length + step - key_pos,
        jnp.where(is_tail, length + step - tail_pos, step - new_pos),
    )
    live_prefix = jnp.logical_and(is_prefix, key_pos < prefix_end)
    live_tail = jnp.logical_and(jnp.logical_and(is_tail, tail_pos < length), own)
    live_new = jnp.logical_and(
        jnp.logical_and(is_new, new_pos <= step), jnp.logical_and(own, core == 0)
    )
    live = jnp.logical_or(live_prefix, jnp.logical_or(live_tail, live_new))
    dist[...] = jnp.where(live, apart.astype(F32), FAR)

    stage[...] = jnp.zeros_like(stage)
    small[1].wait()
    stage[0:steps, :] = nk_in[0].astype(F32)
    kbuf[prefix + tail : keys, :] = stage[...].astype(BF16)
    small[2].wait()
    stage[0:steps, :] = nv_in[0].astype(F32)
    vbuf[prefix + tail : keys, :] = stage[...].astype(BF16)
    small[0].wait()
    for r in range(group_req):
        stage[r * steps : (r + 1) * steps, :] = q_in[r].astype(F32)
    qbuf[...] = stage[...].astype(BF16)
    small[3].wait()
    for r in range(group_req):
        ybuf[r * steps : (r + 1) * steps, :] = resid_in[r].astype(F32)

    wo_load.start()
    wu_load.start()
    wd_load.start()

    pl.semaphore_wait(barrier, N - 1 + G - 1)

    inv_scale = 1.0 / math.sqrt(head_dim)
    lane = lax.broadcasted_iota(jnp.int32, (rows, LANES), 1)
    sub = lax.broadcasted_iota(jnp.int32, (rows, LANES), 0)

    def packed(columns):
        out = jnp.zeros((rows, LANES), F32)
        for c, column in enumerate(columns):
            out = jnp.where(lane == sub + c * rows, column, out)
        return jnp.sum(out, axis=0, keepdims=True)

    def unpacked(line, c):
        return jnp.sum(jnp.where(lane == sub + c * rows, line, 0.0), axis=1, keepdims=True)


    def partials(i, carry):
        pair = [N - 1 - 2 * i, N - 2 - 2 * i]
        for k in pair:
            for load in cache_loads(k):
                load.wait()
        places = [(partner(k), j) for k in pair for j in range(heads)]
        spans = [
            pl.ds(pl.multiple_of(p * block, block) + j * head_dim, head_dim) for p, j in places
        ]
        scores = [
            lax.dot_general(
                qbuf[:, cols], kbuf[:, cols], (((1,), (1,)), ((), ())), preferred_element_type=F32
            )
            for cols in spans
        ]
        scores = [
            member * inv_scale - slopes[p * heads + j] * dist[...]
            for member, (p, j) in zip(scores, places)
        ]
        tops = [
            jnp.maximum(jnp.max(member, axis=1, keepdims=True), FLOOR) for member in scores
        ]
        weights = [jnp.exp(member - top) for member, top in zip(scores, tops)]
        totals = [jnp.sum(member, axis=1, keepdims=True) for member in weights]
        mixed = [
            jnp.dot(member.astype(BF16), vbuf[:, cols], preferred_element_type=F32)
            for member, cols in zip(weights, spans)
        ]
        for half in range(2):
            p = places[half * heads][0]
            for j in range(heads):
                at = half * heads + j
                o_send[p, :, j * head_dim : (j + 1) * head_dim] = mixed[at].astype(BF16)
            span = slice(half * heads, (half + 1) * heads)
            st_send[p] = packed(tops[span] + totals[span])

            @pl.when(pair[half] > 0)
            def _():
                remote(o_send.at[p], o_recv.at[me], o_ss.at[p], o_rs.at[me], peer(p)).start()
                remote(st_send.at[p], st_recv.at[me], st_ss.at[p], st_rs.at[me], peer(p)).start()

        return carry

    lax.fori_loop(0, N // 2, partials, 0)
    o_recv[me] = o_send[me]
    st_recv[me] = st_send[me]

    for k in range(1, N):
        p = lax.rem(me + N - k, N)
        remote(o_send.at[p], o_recv.at[p], o_ss.at[p], o_rs.at[p], peer(p)).wait_recv()
        remote(st_send.at[p], st_recv.at[p], st_ss.at[p], st_rs.at[p], peer(p)).wait_recv()
    stats = [st_recv[i] for i in range(N)]
    best = stats[0]
    for i in range(1, N):
        best = jnp.maximum(best, stats[i])
    factors = [jnp.exp(member - best) for member in stats]
    shift = heads * rows
    upper = lax.broadcasted_iota(jnp.int32, (1, LANES), 1) >= shift
    sums_of = [pltpu.roll(member, shift, 1) for member in stats]
    whole = factors[0] * sums_of[0]
    for i in range(1, N):
        whole = whole + factors[i] * sums_of[i]
    shares = [jnp.where(upper, 0.0, member / jnp.where(upper, 1.0, whole)) for member in factors]
    for j in range(heads):
        cols = slice(j * head_dim, (j + 1) * head_dim)
        mixed = o_recv[0, :, cols].astype(F32) * unpacked(shares[0], j)
        for i in range(1, N):
            mixed = mixed + o_recv[i, :, cols].astype(F32) * unpacked(shares[i], j)
        att[me, :, cols] = mixed.astype(BF16)
    for k in range(N - 1, 0, -1):
        p = partner(k)
        remote(att.at[me], att.at[me], att_ss.at[p], att_rs.at[me], peer(p)).start()

    wo_load.wait()

    def out_proj(k, carry):
        p = partner(k)

        @pl.when(k > 0)
        def _():
            remote(att.at[p], att.at[p], att_ss.at[p], att_rs.at[p], peer(p)).wait_recv()

        piece = pl.ds(pl.multiple_of(p * block, block), block)
        ybuf[...] += jnp.dot(att[p], wo[piece, :], preferred_element_type=F32)
        return carry

    lax.fori_loop(0, N, out_proj, 0)

    y = ybuf[...]
    sums = packed([jnp.sum(y, axis=1, keepdims=True), jnp.sum(y * y, axis=1, keepdims=True)])
    sum_send[...] = sums
    for k in range(N - 1, 0, -1):
        p = partner(k)
        remote(sum_send, sum_recv.at[me], sum_ss.at[p], sum_rs.at[me], peer(p)).start()
    sum_recv[me] = sums
    for k in range(1, N):
        p = lax.rem(me + N - k, N)
        remote(sum_send, sum_recv.at[p], sum_ss.at[p], sum_rs.at[p], peer(p)).wait_recv()
    sums = jnp.sum(sum_recv[...], axis=0)
    mean = unpacked(sums, 0) / width
    var = unpacked(sums, 1) / width - mean * mean
    hidden = (y - mean) * lax.rsqrt(var + 1e-05) * gain_ref[...].astype(F32)[None, :]
    mine = pl.ds(pl.multiple_of(grp * rows, rows), rows)
    hid[mine, :] = hidden.astype(BF16)
    for k in range(1, G):
        g = lax.rem(grp + k, G)
        remote(hid.at[mine], hid.at[mine], hid_ss.at[g], hid_rs.at[grp], {"grp": g}).start()
    wu_load.wait()
    for k in range(1, G):
        g = lax.rem(grp + G - k, G)
        theirs = pl.ds(pl.multiple_of(g * rows, rows), rows)
        remote(hid.at[theirs], hid.at[theirs], hid_ss.at[g], hid_rs.at[g], {"grp": g}).wait_recv()

    other = 1 - core

    def lift(index):
        piece = pl.ds(pl.multiple_of(index * act.shape[2], act.shape[2]), act.shape[2])
        return jnp.dot(hid[...], wu[:, piece], preferred_element_type=F32)

    def pair_blocks(k, carry):
        z = across(S - 1 - k)
        up_send[z] = lift(z * C + other).astype(BF16)
        remote(up_send.at[z], up_pair.at[z], pair_ss.at[z], pair_rs.at[z], {"mlp": other}).start()
        return carry

    lax.fori_loop(0, S, pair_blocks, 0)

    def z_blocks(k, carry):
        z = across(S - 1 - k)
        part = lift(z * C + core)
        remote(
            up_send.at[z], up_pair.at[z], pair_ss.at[z], pair_rs.at[z], {"mlp": other}
        ).wait_recv()
        part = part + up_pair[z].astype(F32)

        @pl.when(k < S - 1)
        def _():
            up_zsend[z] = part.astype(BF16)
            remote(
                up_zsend.at[z], up_zrecv.at[seq], zup_ss.at[z], zup_rs.at[seq], {"seq": z}
            ).start()

        @pl.when(k == S - 1)
        def _():
            acc[...] = part

        return carry

    lax.fori_loop(0, S, z_blocks, 0)
    lifted = acc[...]
    for k in range(1, S):
        z = lax.rem(seq + S - k, S)
        remote(
            up_zsend.at[z], up_zrecv.at[z], zup_ss.at[z], zup_rs.at[z], {"seq": z}
        ).wait_recv()
        lifted = lifted + up_zrecv[z].astype(F32)
    act[me] = (0.5 * lifted * (1.0 + lax.erf(lifted * math.sqrt(0.5)))).astype(BF16)

    for k in range(S - 1, 0, -1):
        z = across(k)
        remote(act.at[me], act.at[me], act_ss.at[z], act_rs.at[me], {"seq": z}).start()
    remote(act.at[me], act.at[me], fwd_ss.at[seq], act_rs.at[me], {"mlp": other}).start()

    wd_load.wait()

    def lower(index):
        piece = pl.ds(pl.multiple_of(index * act.shape[2], act.shape[2]), act.shape[2])
        return jnp.dot(act[index], wd[piece, :], preferred_element_type=F32)

    acc[...] = lower(me)

    def down(k, carry):
        z = across(k)
        near = z * C + core
        far = z * C + other

        @pl.when(k > 0)
        def _():
            remote(act.at[near], act.at[near], act_ss.at[z], act_rs.at[near], {"seq": z}).wait_recv()
            remote(act.at[near], act.at[near], fwd_ss.at[z], act_rs.at[near], {"mlp": other}).start()
            acc[...] += lower(near)

        remote(act.at[far], act.at[far], fwd_ss.at[z], act_rs.at[far], {"mlp": other}).wait_recv()
        acc[...] += lower(far)
        return carry

    lax.fori_loop(0, S, down, 0)

    for k in range(1, G):
        g = lax.rem(grp + k, G)
        theirs = pl.ds(pl.multiple_of(g * rows, rows), rows)
        proj_send[g] = acc[theirs, :].astype(BF16)
        remote(
            proj_send.at[g], proj_recv.at[grp], proj_ss.at[g], proj_rs.at[grp], {"grp": g}
        ).start()
    total = ybuf[...] + acc[mine, :]
    for k in range(1, G):
        g = lax.rem(grp + G - k, G)
        remote(
            proj_send.at[g], proj_recv.at[g], proj_ss.at[g], proj_rs.at[g], {"grp": g}
        ).wait_recv()
        total = total + proj_recv[g].astype(F32)
    ybuf[...] = total
    for r in range(group_req):
        out_ref[r] = ybuf[r * steps : (r + 1) * steps, :]

    for k in range(1, N):
        p = lax.rem(me + k, N)
        remote(o_send.at[p], o_recv.at[me], o_ss.at[p], o_rs.at[me], peer(p)).wait_send()
        remote(st_send.at[p], st_recv.at[me], st_ss.at[p], st_rs.at[me], peer(p)).wait_send()
        remote(att.at[me], att.at[me], att_ss.at[p], att_rs.at[me], peer(p)).wait_send()
        remote(sum_send, sum_recv.at[me], sum_ss.at[p], sum_rs.at[me], peer(p)).wait_send()
    for k in range(1, G):
        g = lax.rem(grp + k, G)
        remote(hid.at[mine], hid.at[mine], hid_ss.at[g], hid_rs.at[grp], {"grp": g}).wait_send()
        remote(
            proj_send.at[g], proj_recv.at[grp], proj_ss.at[g], proj_rs.at[grp], {"grp": g}
        ).wait_send()
    for z in range(S):
        remote(
            up_send.at[z], up_pair.at[z], pair_ss.at[z], pair_rs.at[z], {"mlp": other}
        ).wait_send()
        near = z * C + core
        remote(act.at[near], act.at[near], fwd_ss.at[z], act_rs.at[near], {"mlp": other}).wait_send()
    for k in range(1, S):
        z = lax.rem(seq + k, S)
        remote(
            up_zsend.at[z], up_zrecv.at[seq], zup_ss.at[z], zup_rs.at[seq], {"seq": z}
        ).wait_send()
        remote(act.at[me], act.at[me], act_ss.at[z], act_rs.at[me], {"seq": z}).wait_send()


def fused(
    G,
    S,
    C,
    queries,
    new_keys,
    new_values,
    prefix_keys,
    prefix_values,
    tail_keys,
    tail_values,
    prefix_len,
    tail_len,
    resid,
    w_out,
    ln_gain,
    w_up,
    w_down,
):
    group_req, steps, width = queries.shape
    rows = group_req * steps
    N = S * C
    block = resid.shape[2]
    lifted = w_up.shape[1] // N
    keys = prefix_keys.shape[1] + tail_keys.shape[1] + NEW_PAD
    slopes = jnp.asarray(np.power(2.0, -8.0 * (np.arange(H) + 1.0) / H).astype(np.float32))
    dma = pltpu.SemaphoreType.DMA
    hbm = pl.BlockSpec(memory_space=pl.ANY)
    smem = pl.BlockSpec(memory_space=pltpu.SMEM)
    vmem = pl.BlockSpec(memory_space=pltpu.VMEM)
    return pl.pallas_call(
        functools.partial(layer_kernel, G, S, C),
        out_shape=jax.ShapeDtypeStruct((group_req, steps, block), F32),
        in_specs=[hbm] * 7 + [smem] * 3 + [hbm, vmem] + [hbm] * 3,
        out_specs=vmem,
        scratch_shapes=[
            pltpu.VMEM(queries.shape, BF16),
            pltpu.VMEM(new_keys.shape, BF16),
            pltpu.VMEM(new_values.shape, BF16),
            pltpu.VMEM(resid.shape, BF16),
            pltpu.VMEM((rows, width), F32),
            pltpu.VMEM((rows, width), BF16),
            pltpu.VMEM((keys, width), BF16),
            pltpu.VMEM((keys, width), BF16),
            pltpu.VMEM((rows, keys), F32),
            pltpu.VMEM(w_out.shape, BF16),
            pltpu.VMEM(w_up.shape, BF16),
            pltpu.VMEM(w_down.shape, BF16),
            pltpu.VMEM((N, rows, block), BF16),
            pltpu.VMEM((N, rows, block), BF16),
            pltpu.VMEM((N, 1, LANES), F32),
            pltpu.VMEM((N, 1, LANES), F32),
            pltpu.VMEM((N, rows, block), BF16),
            pltpu.VMEM((rows, block), F32),
            pltpu.VMEM((1, LANES), F32),
            pltpu.VMEM((N, 1, LANES), F32),
            pltpu.VMEM((G * rows, block), BF16),
            pltpu.VMEM((S, G * rows, lifted), BF16),
            pltpu.VMEM((S, G * rows, lifted), BF16),
            pltpu.VMEM((S, G * rows, lifted), BF16),
            pltpu.VMEM((S, G * rows, lifted), BF16),
            pltpu.VMEM((N, G * rows, lifted), BF16),
            pltpu.VMEM((G * rows, block), F32),
            pltpu.VMEM((G, rows, block), BF16),
            pltpu.VMEM((G, rows, block), BF16),
            dma((7,)),
            dma((4, N)),
            dma((N,)),
            dma((N,)),
            dma((N,)),
            dma((N,)),
            dma((N,)),
            dma((N,)),
            dma((N,)),
            dma((N,)),
            dma((G,)),
            dma((G,)),
            dma((S,)),
            dma((S,)),
            dma((S,)),
            dma((S,)),
            dma((S,)),
            dma((S,)),
            dma((N,)),
            dma((G,)),
            dma((G,)),
        ],
        compiler_params=pltpu.CompilerParams(
            collective_id=0, has_side_effects=True, vmem_limit_bytes=63 * 1024 * 1024
        ),
        cost_estimate=pl.CostEstimate(
            flops=2 * rows * width * (keys * 2 + block) + 4 * G * rows * block * w_up.shape[1],
            bytes_accessed=4 * keys * width + 2 * (w_out.size + w_up.size + w_down.size),
            transcendentals=rows * keys * H,
        ),
    )(
        queries,
        new_keys,
        new_values,
        prefix_keys,
        prefix_values,
        tail_keys,
        tail_values,
        prefix_len,
        tail_len,
        slopes,
        resid,
        ln_gain,
        w_out,
        w_up,
        w_down,
    )


def layer_body(mesh):
    G, S, C = (mesh.shape[axis] for axis in ("grp", "seq", "mlp"))

    def run(*args):
        rows = args[0].shape[0] * args[0].shape[1]
        block = args[9].shape[2]
        lifted = args[12].shape[1] // (S * C)
        heads = block // (args[0].shape[2] // H)
        if (S, C) == (4, 2) and 2 * heads * rows == LANES and lifted == block and block % LANES == 0 and rows == NEW_PAD:
            return fused(G, S, C, *args)
        return body(*args)

    return run


def solution(mesh):
    return jax.shard_map(
        layer_body(mesh),
        mesh=mesh,
        in_specs=(
            P("grp", None, None),
            P(("grp", "seq"), None, None),
            P(("grp", "seq"), None, None),
            P("grp", ("seq", "mlp"), None),
            P("grp", ("seq", "mlp"), None),
            P(("grp", "seq"), "mlp", None),
            P(("grp", "seq"), "mlp", None),
            P("grp"),
            P("grp"),
            P("grp", None, ("seq", "mlp")),
            P(None, ("seq", "mlp")),
            P(("seq", "mlp")),
            P(("seq", "mlp"), "grp"),
            P("grp", ("seq", "mlp")),
        ),
        out_specs=P("grp", None, ("seq", "mlp")),
        check_vma=False,
    )
```
